256 devices in a mesh: gx: 16 (over z_lo, y, core), gy: 16 (over z_hi, x).
Axes of the slice: x: 4, y: 4, z: 8 (z_hi: 4, z_lo: 2; z = z_hi * 2 + z_lo), core: 2. Of those that a mesh axis runs over, the one named last changes fastest.
Arguments:
- adjoint_start: float32 [128, 128, 16, 320], P('gx', 'gy'), may hold values from -6 to 6
- source: float32 [128, 128, 16, 320], P('gx', 'gy'), may hold values from -6 to 6
- self_scale: bfloat16 [128, 128, 16, 320], P('gx', 'gy'), may hold values from 0.25 to 1.75
- relax_scale: bfloat16 [128, 128, 16, 320], P('gx', 'gy'), may hold values from 0.29882812 to 1
- face_scale: bfloat16 [6, 128, 128, 16, 320], P(None, 'gx', 'gy'), may hold values from 0.049804688 to 0.59765625
- self_block: bfloat16 [320, 320], replicated, may hold values from -0.3125 to 0.3125
- face_block: bfloat16 [6, 320, 320], replicated, may hold values from -0.3125 to 0.3125
- inverse_block: bfloat16 [320, 320], replicated, may hold values from -0.3125 to 0.3125
- shape_basis: bfloat16 [320, 128], replicated, may hold values from -0.3125 to 0.3125
- wall_elem: int32 [16, 16, 256], P('gx', 'gy'), may hold values from 0 to 1023, as said below
- wall_owner: int32 [16, 16, 256], P('gx', 'gy'), may hold values from 0 to 2048, as said below
- wall_area: float32 [16, 16, 256], P('gx', 'gy'), may hold values from 0.2 to 2
Outputs:
- adjoint: float32 [128, 128, 16, 320], P('gx', 'gy')
- patch_gradient: float32 [2048, 128], P(('gx', 'gy'))
The draws below stay inside these ranges and needn't reach their ends.
Inputs may be any that keep to these rules, and one draw needn't show every extreme that they name: `wall_elem`: distinct local element indices within each device's tile. `wall_owner`: 2048 marks an empty slot; live slots come first in each tile; each tile has at most 256 live slots, some tile exactly 256; patch p lies in streamwise group p // (8 * 16), and in each tile at most 16 live slots name patches of one streamwise group, some tile exactly 16.
All inputs are finite; a program needn't handle non-finite values.
Results may differ from the reference program's by a relative error of at most 0.007.
Values may be sent and summed in bfloat16 or wider, within the bound.
A program may use at most 64 MiB of HBM per device.

```python
import math
import jax
import jax.numpy as jnp

BW = 320
GW = 128
EX = 8
EY = 8
EZ = 16
ITERS = 2
WMAX = 256
P_DEV = 8
NX = 128
NY = 128
PATCHES = 2048
WCAP = 16
N_GX = 16
N_GY = 16


def draw_wall_elem(key, part):
    count = EX * EY * EZ
    scores = jax.random.randint(key, (N_GX, N_GY, count), 0, 65536) * count + jnp.arange(count, dtype=jnp.int32)
    order = jnp.argsort(scores, axis=-1, stable=True).astype(jnp.int32)
    return order[:, :, :WMAX]


def draw_wall_owner(key, part):
    tiles = N_GX * N_GY
    lowest = max(1, WMAX // 4)
    groups_used = WMAX // WCAP
    per_group = P_DEV * N_GY
    live = jax.random.randint(jax.random.fold_in(key, 7), (tiles,), lowest, WMAX + 1)
    chosen = jax.random.randint(jax.random.fold_in(key, 8), (), 0, tiles)
    live = live.at[chosen].set(WMAX)
    live = live.at[(chosen + 1) % tiles].set(lowest)
    offset = jax.random.randint(jax.random.fold_in(key, 10), (tiles, 1), 0, N_GX)
    slots = jnp.arange(WMAX, dtype=jnp.int32)[None, :]
    group = (offset + slots % groups_used) % N_GX
    within = jax.random.randint(jax.random.fold_in(key, 9), (tiles, WMAX), 0, per_group)
    owners = group * per_group + within
    owners = jnp.where(slots < live[:, None], owners, PATCHES)
    return owners.reshape(N_GX, N_GY, WMAX).astype(jnp.int32)


def level_of(key, shape, cuts, least, top_value):
    loudness = 1.0
    for dim, blocks in cuts:
        heights = jax.random.uniform(jax.random.fold_in(jax.random.fold_in(key, 6), dim), (blocks,), jnp.float32, least / len(cuts), top_value / len(cuts))
        loudness = loudness * jnp.repeat(jnp.exp(heights), shape[dim] // blocks).reshape((-1,) + (1,) * (len(shape) - 1 - dim))
    return loudness


def bell_draw(rng, dims, scale, bound, shards=(), kind=jnp.bfloat16):
    result = jax.random.normal(rng, dims, jnp.float32) * scale
    if len(shards) > 0:
        result = level_of(rng, dims, shards, -0.22, 0.18) * result
    return jnp.clip(result, min=-bound, max=bound).astype(kind)


def setup_inputs(seed: int = 0) -> dict:
    keys = jax.random.split(jax.random.key(seed), 13)
    return {
        "adjoint_start": bell_draw(keys[0], (NX, NY, EZ, BW), 1.0, 6.0, ((0, 16), (1, 16)), jnp.float32),
        "source": bell_draw(keys[1], (NX, NY, EZ, BW), 1.0, 6.0, ((0, 16), (1, 16)), jnp.float32),
        "self_scale": jnp.clip(1.0 + 0.15 * jax.random.normal(keys[2], (NX, NY, EZ, BW), jnp.float32), 0.25, 1.75).astype(jnp.bfloat16),
        "relax_scale": jnp.clip(jnp.exp(math.log(1.0) - 1.2078867 * jax.random.uniform(keys[3], (NX, NY, EZ, BW), jnp.float32) ** level_of(keys[3], (NX, NY, EZ, BW), ((0, 16), (1, 16)), -0.2, 0.2)), 0.29882812, 1.0).astype(jnp.bfloat16),
        "face_scale": jnp.clip(0.049804688 + 0.54785156 * jax.random.uniform(keys[4], (6, NX, NY, EZ, BW), jnp.float32) ** level_of(keys[4], (6, NX, NY, EZ, BW), ((1, 16), (2, 16)), -0.2, 0.2), 0.049804688, 0.59765625).astype(jnp.bfloat16),
        "self_block": bell_draw(keys[5], (BW, BW), BW ** -0.5, 0.3125),
        "face_block": bell_draw(keys[6], (6, BW, BW), BW ** -0.5, 0.3125),
        "inverse_block": bell_draw(keys[7], (BW, BW), BW ** -0.5, 0.3125),
        "shape_basis": bell_draw(keys[8], (BW, GW), BW ** -0.5, 0.3125),
        "wall_elem": draw_wall_elem(jax.random.fold_in(keys[12], 71), 0),
        "wall_owner": draw_wall_owner(jax.random.fold_in(keys[12], 71), 0),
        "wall_area": jnp.clip(jnp.exp(math.log(2.0) - 2.3025851 * jax.random.uniform(keys[11], (N_GX, N_GY, WMAX), jnp.float32) ** level_of(keys[11], (N_GX, N_GY, WMAX), ((0, 16), (1, 16)), -0.2, 0.2)), 0.2, 2.0),
    }


def neighbours(rounded):
    padded = jnp.pad(rounded, ((1, 1), (1, 1), (1, 1), (0, 0)))
    inner = padded
    return [inner[:-2, 1:-1, 1:-1], inner[2:, 1:-1, 1:-1], inner[1:-1, :-2, 1:-1], inner[1:-1, 2:, 1:-1], inner[1:-1, 1:-1, :-2], inner[1:-1, 1:-1, 2:]]


def reference(adjoint_start, source, self_scale, relax_scale, face_scale, self_block, face_block, inverse_block, shape_basis, wall_elem, wall_owner, wall_area):
    adjoint = adjoint_start
    for step in range(ITERS):
        rounded = adjoint.astype(jnp.bfloat16)
        residual = source - self_scale * jnp.dot(rounded, self_block, preferred_element_type=jnp.float32)
        faces = neighbours(rounded)
        for face in range(6):
            residual = residual - face_scale[face] * jnp.dot(faces[face], face_block[face], preferred_element_type=jnp.float32)
        update = (relax_scale * residual).astype(jnp.bfloat16)
        adjoint = adjoint + jnp.dot(update, inverse_block, preferred_element_type=jnp.float32)
    final = adjoint.astype(jnp.bfloat16)
    tiles = final.reshape(N_GX, EX, N_GY, EY, EZ, BW).transpose(0, 2, 1, 3, 4, 5).reshape(N_GX, N_GY, EX * EY * EZ, BW)
    picked = jnp.take_along_axis(tiles, wall_elem.astype(jnp.int32)[:, :, :, None], axis=2)
    proj = jnp.dot(picked.reshape(-1, BW), shape_basis, preferred_element_type=jnp.float32)
    wall_row = (proj * wall_area.reshape(-1, 1)).astype(jnp.bfloat16)
    summed = jax.ops.segment_sum(wall_row.astype(jnp.float32), wall_owner.reshape(-1).astype(jnp.int32), num_segments=PATCHES + 1)
    return adjoint, summed[:PATCHES]
```

```python
import functools

import jax
import jax.numpy as jnp
from jax import lax
from jax.experimental import pallas as pl
from jax.experimental.pallas import tpu as pltpu
from jax.sharding import PartitionSpec as P

ITERS = 2
P_DEV = 8
CAP = 16
MESH = pl.DeviceIdType.MESH
F32 = jnp.float32
BF16 = jnp.bfloat16


def kernel(
    nx,
    ny,
    ex,
    ey,
    ez,
    adj_hbm,
    src_hbm,
    ss_hbm,
    rx_hbm,
    fs_hbm,
    sb_hbm,
    fb_hbm,
    ib_hbm,
    basis_hbm,
    elem_hbm,
    owner_hbm,
    area_hbm,
    out_hbm,
    grad_ref,
    adj,
    src,
    ss,
    rx,
    fs,
    sb,
    fb,
    ib,
    basis,
    elem,
    owner,
    area,
    halo,
    pick,
    meta_out,
    meta_in,
    rows_out,
    rows_in,
    sums_out,
    sums_in,
    adj_sem,
    plane_sem,
    block_sem,
    wall_sem,
    out_sem,
    x_send,
    x_recv,
    y_send,
    y_recv,
    meta_send,
    meta_recv,
    rows_send,
    rows_recv,
    sums_send,
    sums_recv,
):
    gx, gy = lax.axis_index("gx"), lax.axis_index("gy")
    plane = ey * ez
    pairs = ex // 2
    width = adj.shape[2]
    group = P_DEV * ny
    slots = elem.shape[1]
    sorted_slots = nx * CAP

    adj_copies = [
        pltpu.make_async_copy(
            adj_hbm.at[pl.ds(2 * k, 2)], adj.at[pl.ds(2 * k, 2)], adj_sem.at[k]
        )
        for k in range(pairs)
    ]
    wall_copies = [
        pltpu.make_async_copy(a, b, wall_sem.at[i])
        for i, (a, b) in enumerate(
            ((elem_hbm, elem), (owner_hbm, owner), (area_hbm, area))
        )
    ]
    block_copies = [
        pltpu.make_async_copy(a, b, block_sem.at[i])
        for i, (a, b) in enumerate(
            ((sb_hbm, sb), (fb_hbm, fb), (ib_hbm, ib), (basis_hbm, basis))
        )
    ]

    def plane_copies(p, k):
        rows = pl.ds(p, 2)
        return [
            pltpu.make_async_copy(src_hbm.at[rows], src.at[rows], plane_sem.at[k, 0]),
            pltpu.make_async_copy(ss_hbm.at[rows], ss.at[rows], plane_sem.at[k, 1]),
            pltpu.make_async_copy(rx_hbm.at[rows], rx.at[rows], plane_sem.at[k, 2]),
            pltpu.make_async_copy(
                fs_hbm.at[:, rows], fs.at[:, rows], plane_sem.at[k, 3]
            ),
        ]

    order = [0, pairs - 1, *range(1, pairs - 1)]

    def place(k):
        return jnp.where(k == 0, 0, jnp.where(k == 1, pairs - 1, k - 1))

    for c in adj_copies + wall_copies + block_copies:
        c.start()
    for k, p in enumerate(order):
        for c in plane_copies(2 * p, k):
            c.start()

    if nx * ny > 1:
        barrier = pltpu.get_barrier_semaphore()

        @pl.loop(1, nx)
        def _(d):
            pl.semaphore_signal(
                barrier,
                inc=1,
                device_id=(lax.rem(gx + d, nx), gy),
                device_id_type=MESH,
            )

        @pl.loop(1, ny)
        def _(d):
            pl.semaphore_signal(
                barrier,
                inc=1,
                device_id=(gx, lax.rem(gy + d, ny)),
                device_id_type=MESH,
            )

    zx = jnp.zeros((1, plane, width), BF16)
    zy = jnp.zeros((ex, ez, width), BF16)
    for it in range(ITERS):

        @pl.when(gx == 0)
        def _():
            halo[it, 0:1, ez : ez + plane] = zx

        @pl.when(gx == nx - 1)
        def _():
            halo[it, ex + 1 : ex + 2, ez : ez + plane] = zx

        @pl.when(gy == 0)
        def _():
            halo[it, 1 : ex + 1, 0:ez] = zy

        @pl.when(gy == ny - 1)
        def _():
            halo[it, 1 : ex + 1, ez + plane : 2 * ez + plane] = zy

    for c in adj_copies:
        c.wait()
    for k in range(pairs):
        halo[0, 1 + 2 * k : 3 + 2 * k, ez : ez + plane] = adj[
            2 * k : 2 * k + 2
        ].astype(BF16)

    def x_copies(it):
        mid = pl.ds(ez, plane)
        up = pltpu.make_async_remote_copy(
            halo.at[it, ex, mid],
            halo.at[it, 0, mid],
            x_send.at[it, 0],
            x_recv.at[it, 0],
            device_id=(jnp.minimum(gx + 1, nx - 1), gy),
            device_id_type=MESH,
        )
        down = pltpu.make_async_remote_copy(
            halo.at[it, 1, mid],
            halo.at[it, ex + 1, mid],
            x_send.at[it, 1],
            x_recv.at[it, 1],
            device_id=(jnp.maximum(gx - 1, 0), gy),
            device_id_type=MESH,
        )
        return up, down

    def y_copies(it, start, count, k):
        rows = pl.ds(start + 1, count)
        up = pltpu.make_async_remote_copy(
            halo.at[it, rows, pl.ds(plane, ez)],
            halo.at[it, rows, pl.ds(0, ez)],
            y_send.at[k, 0],
            y_recv.at[k, 0],
            device_id=(gx, jnp.minimum(gy + 1, ny - 1)),
            device_id_type=MESH,
        )
        down = pltpu.make_async_remote_copy(
            halo.at[it, rows, pl.ds(ez, ez)],
            halo.at[it, rows, pl.ds(plane + ez, ez)],
            y_send.at[k, 1],
            y_recv.at[k, 1],
            device_id=(gx, jnp.maximum(gy - 1, 0)),
            device_id_type=MESH,
        )
        return up, down

    def send(pair, coord, size):
        up, down = pair

        @pl.when(coord < size - 1)
        def _():
            up.start()

        @pl.when(coord > 0)
        def _():
            down.start()

    def arrive(pair, coord, size):
        up, down = pair

        @pl.when(coord > 0)
        def _():
            up.wait_recv()

        @pl.when(coord < size - 1)
        def _():
            down.wait_recv()

    def sent(pair, coord, size):
        up, down = pair

        @pl.when(coord < size - 1)
        def _():
            up.wait_send()

        @pl.when(coord > 0)
        def _():
            down.wait_send()

    if nx * ny > 1:
        pl.semaphore_wait(barrier, nx + ny - 2)
    send(x_copies(0), gx, nx)
    send(y_copies(0, 0, ex, pairs), gy, ny)

    for c in wall_copies:
        c.wait()
    owner_row = owner[...]
    group_row = owner_row // group
    g_row = group_row.astype(F32)
    sub = lax.broadcasted_iota(jnp.int32, (slots, slots), 0)
    lane = lax.broadcasted_iota(jnp.int32, (slots, slots), 1)
    g_col = jnp.sum(jnp.where(sub == lane, g_row, 0.0), axis=1, keepdims=True)
    before = jnp.where((g_col == g_row) & (sub < lane), 1.0, 0.0)
    rank_row = jnp.sum(before, axis=0, keepdims=True)
    key_row = g_row * CAP + rank_row
    to = lax.broadcasted_iota(jnp.int32, (sorted_slots, slots), 0).astype(F32)
    perm = to == key_row
    elem_row = elem[...].astype(F32) + 1.0
    elem_col = jnp.sum(jnp.where(perm, elem_row, 0.0), axis=1, keepdims=True) - 1.0
    area_col = jnp.sum(jnp.where(perm, area[...], 0.0), axis=1, keepdims=True)
    local_row = (owner_row - group_row * group - group).astype(F32)
    local_col = jnp.sum(jnp.where(perm, local_row, 0.0), axis=1, keepdims=True) + group
    meta_out[...] = (
        jnp.broadcast_to(local_col, (sorted_slots, 128))
        .astype(BF16)
        .reshape(nx, CAP, 128)
    )
    for p in range(ex):
        at = lax.broadcasted_iota(jnp.int32, (sorted_slots, plane), 1) + p * plane
        pick[:, p * plane : (p + 1) * plane] = jnp.where(
            elem_col == at.astype(F32), 1.0, 0.0
        ).astype(BF16)

    def to_x(out, into, send_sem, recv_sem, d):
        peer = lax.rem(gx + d, nx)
        return pltpu.make_async_remote_copy(
            out.at[peer],
            into.at[gx],
            send_sem.at[d],
            recv_sem.at[d],
            device_id=(peer, gy),
            device_id_type=MESH,
        )

    def to_y(d):
        peer = lax.rem(gy + d, ny)
        return pltpu.make_async_remote_copy(
            sums_out.at[peer],
            sums_in.at[gy],
            sums_send.at[d],
            sums_recv.at[d],
            device_id=(gx, peer),
            device_id_type=MESH,
        )

    @pl.loop(1, nx)
    def _(d):
        to_x(meta_out, meta_in, meta_send, meta_recv, d).start()

    meta_in[gx] = meta_out[gx]

    for c in block_copies:
        c.wait()
    arrive(x_copies(0), gx, nx)
    arrive(y_copies(0, 0, ex, pairs), gy, ny)

    iz = lax.rem(lax.broadcasted_iota(jnp.int32, (2 * plane, width), 0), ez)

    def dot(a, b):
        return jnp.dot(a, b, preferred_element_type=F32)

    def out_copy(p, k):
        return pltpu.make_async_copy(
            adj.at[pl.ds(p, 2)], out_hbm.at[pl.ds(p, 2)], out_sem.at[k]
        )

    @pl.loop(0, ITERS * pairs)
    def _(t):
        it = t // pairs
        k = t - it * pairs
        p = 2 * place(k)

        @pl.when(it == 0)
        def _():
            for c in plane_copies(p, k):
                c.wait()

        @pl.when(it == 1)
        def _():
            arrive(y_copies(1, p, 2, k), gy, ny)

        up, down = x_copies(1)

        @pl.when((it == 1) & (k == 0) & (gx > 0))
        def _():
            up.wait_recv()

        @pl.when((it == 1) & (k == 1) & (gx < nx - 1))
        def _():
            down.wait_recv()

        def flat(x):
            return x.reshape(2 * plane, width)

        own = flat(adj[pl.ds(p, 2)])
        mid = pl.ds(ez, plane)
        zero = jnp.zeros_like(own)
        faces = [
            flat(halo[it, pl.ds(p, 2), mid]),
            flat(halo[it, pl.ds(p + 2, 2), mid]),
            flat(halo[it, pl.ds(p + 1, 2), pl.ds(0, plane)]),
            flat(halo[it, pl.ds(p + 1, 2), pl.ds(2 * ez, plane)]),
            jnp.where(iz == 0, zero, pltpu.roll(own, 1, 0)).astype(BF16),
            jnp.where(iz == ez - 1, zero, pltpu.roll(own, 2 * plane - 1, 0)).astype(
                BF16
            ),
        ]
        rows = pl.ds(p, 2)
        total = flat(src[rows]) - flat(ss[rows]).astype(F32) * dot(
            own.astype(BF16), sb[...]
        )
        for f in range(6):
            total = total - flat(fs[f, rows]).astype(F32) * dot(faces[f], fb[f])
        update = (flat(rx[rows]).astype(F32) * total).astype(BF16)
        new = (own + dot(update, ib[...])).reshape(2, plane, width)
        adj[rows] = new
        halo[it + 1, pl.ds(p + 1, 2), mid] = new.astype(BF16)

        @pl.when(it == 0)
        def _():
            send(y_copies(1, p, 2, k), gy, ny)

        @pl.when((it == 0) & (k == 1) & (gx < nx - 1))
        def _():
            up.start()

        @pl.when((it == 0) & (k == 0) & (gx > 0))
        def _():
            down.start()

        @pl.when(it == 1)
        def _():
            out_copy(p, k).start()

    picked = jnp.zeros((sorted_slots, width), F32)
    for p in range(0, ex, 2):
        picked = picked + dot(
            pick[:, p * plane : (p + 2) * plane],
            halo[ITERS, p + 1 : p + 3, ez : ez + plane].reshape(2 * plane, width),
        )
    proj = dot(picked.astype(BF16), basis[...])
    rows_out[...] = (proj * area_col).astype(BF16).reshape(nx, CAP, -1)

    @pl.loop(1, nx)
    def _(d):
        to_x(rows_out, rows_in, rows_send, rows_recv, d).start()

    rows_in[gx] = rows_out[gx]

    @pl.loop(1, nx)
    def _(d):
        to_x(meta_out, meta_in, meta_send, meta_recv, d).wait_recv()

    patch = lax.broadcasted_iota(jnp.int32, (sorted_slots, 128), 1).astype(F32)
    mark = jnp.where(
        meta_in[...].reshape(sorted_slots, 128).astype(F32) == patch, 1.0, 0.0
    ).astype(BF16)

    @pl.loop(1, nx)
    def _(d):
        to_x(rows_out, rows_in, rows_send, rows_recv, d).wait_recv()

    sums = lax.dot_general(
        mark,
        rows_in[...].reshape(sorted_slots, -1),
        (((0,), (0,)), ((), ())),
        preferred_element_type=F32,
    )
    sums_out[...] = sums[:group].reshape(ny, P_DEV, -1)

    @pl.loop(1, ny)
    def _(d):
        to_y(d).start()

    sums_in[gy] = sums_out[gy]

    @pl.loop(1, ny)
    def _(d):
        to_y(d).wait_recv()

    grad_ref[...] = jnp.sum(sums_in[...], axis=0)

    for k, p in enumerate(order):
        out_copy(2 * p, k).wait()
    for it in range(ITERS):
        sent(x_copies(it), gx, nx)
    sent(y_copies(0, 0, ex, pairs), gy, ny)
    for k, p in enumerate(order):
        sent(y_copies(1, 2 * p, 2, k), gy, ny)

    @pl.loop(1, nx)
    def _(d):
        to_x(meta_out, meta_in, meta_send, meta_recv, d).wait_send()
        to_x(rows_out, rows_in, rows_send, rows_recv, d).wait_send()

    @pl.loop(1, ny)
    def _(d):
        to_y(d).wait_send()


def local(nx, ny, adjoint, source, ss, rx, fs, sb, fb, ib, basis, elem, owner, area):
    ex, ey, ez, width = adjoint.shape
    plane, pairs = ey * ez, ex // 2
    slots = elem.shape[2]
    params = basis.shape[1]
    planes = (ex, plane, width)
    vmem, dma = pltpu.VMEM, pltpu.SemaphoreType.DMA
    anywhere = pl.BlockSpec(memory_space=pl.ANY)
    out, grad = pl.pallas_call(
        functools.partial(kernel, nx, ny, ex, ey, ez),
        out_shape=(
            jax.ShapeDtypeStruct(planes, F32),
            jax.ShapeDtypeStruct((P_DEV, params), F32),
        ),
        in_specs=[anywhere] * 12,
        out_specs=(anywhere, pl.BlockSpec(memory_space=pltpu.VMEM)),
        scratch_shapes=[
            vmem(planes, F32),
            vmem(planes, F32),
            vmem(planes, BF16),
            vmem(planes, BF16),
            vmem((6, *planes), BF16),
            vmem(sb.shape, BF16),
            vmem(fb.shape, BF16),
            vmem(ib.shape, BF16),
            vmem(basis.shape, BF16),
            vmem((1, slots), jnp.int32),
            vmem((1, slots), jnp.int32),
            vmem((1, slots), F32),
            vmem((ITERS + 1, ex + 2, plane + 2 * ez, width), BF16),
            vmem((nx * CAP, ex * plane), BF16),
            vmem((nx, CAP, 128), BF16),
            vmem((nx, CAP, 128), BF16),
            vmem((nx, CAP, params), BF16),
            vmem((nx, CAP, params), BF16),
            vmem((ny, P_DEV, params), F32),
            vmem((ny, P_DEV, params), F32),
            dma((pairs,)),
            dma((pairs, 4)),
            dma((4,)),
            dma((3,)),
            dma((pairs,)),
            dma((ITERS, 2)),
            dma((ITERS, 2)),
            dma((pairs + 1, 2)),
            dma((pairs + 1, 2)),
            dma((nx,)),
            dma((nx,)),
            dma((nx,)),
            dma((nx,)),
            dma((ny,)),
            dma((ny,)),
        ],
        compiler_params=pltpu.CompilerParams(
            collective_id=0 if nx * ny > 1 else None,
            has_side_effects=True,
            vmem_limit_bytes=62 * 1024 * 1024,
        ),
        name="sweeps",
    )(
        adjoint.reshape(planes),
        source.reshape(planes),
        ss.reshape(planes),
        rx.reshape(planes),
        fs.reshape(6, *planes),
        sb,
        fb,
        ib,
        basis,
        elem.reshape(1, slots),
        owner.reshape(1, slots),
        area.reshape(1, slots),
    )
    return out.reshape(adjoint.shape), grad


def solution(mesh):
    return jax.shard_map(
        functools.partial(local, mesh.shape["gx"], mesh.shape["gy"]),
        mesh=mesh,
        in_specs=(
            P("gx", "gy", None, None),
            P("gx", "gy", None, None),
            P("gx", "gy", None, None),
            P("gx", "gy", None, None),
            P(None, "gx", "gy", None, None),
            P(),
            P(),
            P(),
            P(),
            P("gx", "gy", None),
            P("gx", "gy", None),
            P("gx", "gy", None),
        ),
        out_specs=(P("gx", "gy", None, None), P(("gx", "gy"), None)),
        check_vma=False,
    )
```

```python
import functools

import jax
import jax.numpy as jnp
from jax import lax
from jax.experimental import pallas as pl
from jax.experimental.pallas import tpu as pltpu
from jax.sharding import PartitionSpec as P

ITERS = 2
P_DEV = 8
CAP = 16
CUTS = 2
LANES = 128
MESH = pl.DeviceIdType.MESH
F32 = jnp.float32
BF16 = jnp.bfloat16


def offsets(n, parts):
    if n != functools.reduce(lambda a, b: a * b, (size for size, _ in parts), 1):
        parts = ((n, 1),)
    steps = [()]
    for size, _ in parts:
        steps = [(*o, d) for o in steps for d in range(size)]

    def far(o):
        return sum(min(d, m - d) * hops for d, (m, hops) in zip(o, parts))

    return parts, sorted([o for o in steps if any(o)], key=lambda o: -far(o))


def peers(me, n, parts):
    parts, steps = offsets(n, parts)
    coords, rest = [], me
    for size, _ in reversed(parts):
        coords.insert(0, lax.rem(rest, size))
        rest = rest // size
    out = []
    for o in steps:
        peer = 0
        for c, d, (size, _) in zip(coords, o, parts):
            peer = peer * size + (lax.rem(c + d, size) if d else c)
        out.append(peer)
    return out


def kernel(
    nx,
    ny,
    ex,
    ey,
    ez,
    adj_hbm,
    src_hbm,
    ss_hbm,
    rx_hbm,
    fs_hbm,
    sb_hbm,
    fb_hbm,
    ib_hbm,
    basis_hbm,
    elem_hbm,
    owner_hbm,
    area_hbm,
    out_hbm,
    grad_ref,
    adj,
    src,
    ss,
    rx,
    fs,
    sb,
    fb,
    ib,
    basis,
    elem,
    owner,
    area,
    near,
    total,
    ends,
    end_out,
    x_out,
    x_halo,
    y_out,
    y_halo,
    pick,
    meta_out,
    meta_in,
    rows_out,
    rows_in,
    sums_out,
    sums_in,
    adj_sem,
    plane_sem,
    block_sem,
    wall_sem,
    out_sem,
    x_send,
    x_recv,
    y_send,
    y_recv,
    meta_send,
    meta_recv,
    rows_send,
    rows_recv,
    sums_send,
    sums_recv,
):
    gx, gy = lax.axis_index("gx"), lax.axis_index("gy")
    plane = ey * ez
    depth = ex // CUTS
    deep = depth * plane
    width = adj.shape[2]
    body = width // 256 * 256
    tail = width - body
    group = P_DEV * ny
    slots = elem.shape[1]
    sorted_slots = nx * CAP
    mid = pl.ds(ez, plane)
    x_peers = peers(gx, nx, ((2, 1), (4, 1), (2, 0.1)))
    y_peers = peers(gy, ny, ((4, 2), (4, 1)))

    low, high = pl.ds(0, ez), pl.ds(plane - ez, ez)
    inner = pl.ds(ez, plane - 2 * ez)
    adj_copies = [
        pltpu.make_async_copy(adj_hbm.at[:, a], adj.at[:, a], adj_sem.at[i])
        for i, a in enumerate((low, high, inner))
    ]
    wall_copies = [
        pltpu.make_async_copy(a, b, wall_sem.at[i])
        for i, (a, b) in enumerate(
            ((elem_hbm, elem), (owner_hbm, owner), (area_hbm, area))
        )
    ]
    block_copies = [
        pltpu.make_async_copy(a, b, block_sem.at[i])
        for i, (a, b) in enumerate(
            ((sb_hbm, sb), (fb_hbm, fb), (ib_hbm, ib), (basis_hbm, basis))
        )
    ]

    src_copy = pltpu.make_async_copy(src_hbm, src, plane_sem.at[0])
    ss_copy = pltpu.make_async_copy(ss_hbm, ss, plane_sem.at[1])
    rx_copy = pltpu.make_async_copy(rx_hbm, rx, plane_sem.at[2])
    fs_copies = [
        pltpu.make_async_copy(fs_hbm.at[f], fs.at[f], plane_sem.at[3 + f])
        for f in range(6)
    ]
    face_order = (4, 5, 0, 1, 2, 3)

    areas = (
        ((pl.ds(1, ex - 2), inner),),
        ((pl.ds(0, 1), inner), (pl.ds(ex - 1, 1), inner)),
        ((pl.ds(0, ex), low), (pl.ds(0, ex), high)),
    )

    for c in [*adj_copies, *block_copies, *wall_copies, ss_copy, src_copy]:
        c.start()

    if nx * ny > 1:
        barrier = pltpu.get_barrier_semaphore()
        for peer in x_peers:
            pl.semaphore_signal(
                barrier, inc=1, device_id=(peer, gy), device_id_type=MESH
            )
        for peer in y_peers:
            pl.semaphore_signal(
                barrier, inc=1, device_id=(gx, peer), device_id_type=MESH
            )

    zeros = jnp.zeros((ex, ez, width), BF16)
    near[0, mid] = jnp.zeros((plane, width), BF16)
    near[ex + 1, mid] = jnp.zeros((plane, width), BF16)
    near[1 : ex + 1, 0:ez] = zeros
    near[1 : ex + 1, ez + plane : 2 * ez + plane] = zeros
    end_zeros = jnp.zeros((ex, ez, 256), F32)
    end_out[0, mid, 0:256] = jnp.zeros((plane, 256), F32)
    end_out[ex + 1, mid, 0:256] = jnp.zeros((plane, 256), F32)
    end_out[1 : ex + 1, 0:ez, 0:256] = end_zeros
    end_out[1 : ex + 1, ez + plane : 2 * ez + plane, 0:256] = end_zeros
    rows_x = plane * width // LANES
    rows_y = ex * ez * width // LANES
    for it in range(ITERS):

        @pl.when(gx == 0)
        def _():
            x_halo[it, 0] = jnp.zeros((rows_x, LANES), BF16)

        @pl.when(gx == nx - 1)
        def _():
            x_halo[it, 1] = jnp.zeros((rows_x, LANES), BF16)

        @pl.when(gy == 0)
        def _():
            y_halo[it, 0] = jnp.zeros((rows_y, LANES), BF16)

        @pl.when(gy == ny - 1)
        def _():
            y_halo[it, 1] = jnp.zeros((rows_y, LANES), BF16)

    def pack(ref, x):
        n = x.shape[0]
        for j in range(body // LANES):
            ref[j * n : (j + 1) * n] = x[:, j * LANES : (j + 1) * LANES]
        end = x[:, body:width]
        ref[body // LANES * n : width * n // LANES] = jnp.concatenate(
            [end[: n // 2], end[n // 2 :]], axis=1
        )

    def unpack(ref, n):
        end = ref[body // LANES * n : width * n // LANES]
        return jnp.concatenate(
            [ref[j * n : (j + 1) * n] for j in range(body // LANES)]
            + [jnp.concatenate([end[:, 0:tail], end[:, tail : 2 * tail]], axis=0)],
            axis=1,
        )

    def sides(it, out, into, send_sem, recv_sem, ids):
        return [
            pltpu.make_async_remote_copy(
                out.at[it, i],
                into.at[it, i],
                send_sem.at[it, i],
                recv_sem.at[it, i],
                device_id=d,
                device_id_type=MESH,
            )
            for i, d in enumerate(ids)
        ]

    def x_sides(it):
        ids = ((jnp.minimum(gx + 1, nx - 1), gy), (jnp.maximum(gx - 1, 0), gy))
        return sides(it, x_out, x_halo, x_send, x_recv, ids)

    def y_sides(it):
        ids = ((gx, jnp.minimum(gy + 1, ny - 1)), (gx, jnp.maximum(gy - 1, 0)))
        return sides(it, y_out, y_halo, y_send, y_recv, ids)

    def send(it, make, me, n):
        up, down = make(it)
        pl.when(me < n - 1)(up.start)
        pl.when(me > 0)(down.start)

    def sent(it, make, me, n):
        up, down = make(it)
        pl.when(me < n - 1)(up.wait_send)
        pl.when(me > 0)(down.wait_send)

    def arrive(it, make, me, n):
        up, down = make(it)
        pl.when(me > 0)(up.wait_recv)
        pl.when(me < n - 1)(down.wait_recv)

    def send_x(it, first, final):
        pack(x_out.at[it, 0], final)
        pack(x_out.at[it, 1], first)
        send(it, x_sides, gx, nx)

    def send_y(it, first, final):
        pack(y_out.at[it, 0], final)
        pack(y_out.at[it, 1], first)
        send(it, y_sides, gy, ny)

    strip = (ex * ez, width)
    adj_copies[0].wait()
    adj_copies[1].wait()
    if nx * ny > 1:
        pl.semaphore_wait(barrier, nx + ny - 2)
    send_y(
        0,
        adj[:, low].astype(BF16).reshape(strip),
        adj[:, high].astype(BF16).reshape(strip),
    )
    adj_copies[2].wait()
    send_x(0, adj[0].astype(BF16), adj[ex - 1].astype(BF16))
    for c in [fs_copies[4], fs_copies[5], fs_copies[0]]:
        c.start()
    for k in range(CUTS):
        near[1 + depth * k : 1 + depth * (k + 1), mid] = adj[
            depth * k : depth * (k + 1)
        ].astype(BF16)

    for c in wall_copies:
        c.wait()
    owner_row = owner[...]
    group_row = owner_row // group
    g_row = group_row.astype(F32)
    sub = lax.broadcasted_iota(jnp.int32, (slots, slots), 0)
    lane = lax.broadcasted_iota(jnp.int32, (slots, slots), 1)
    g_col = jnp.sum(jnp.where(sub == lane, g_row, 0.0), axis=1, keepdims=True)
    before = jnp.where((g_col == g_row) & (sub < lane), 1.0, 0.0)
    rank_row = jnp.sum(before, axis=0, keepdims=True)
    key_row = g_row * CAP + rank_row
    to = lax.broadcasted_iota(jnp.int32, (sorted_slots, slots), 0).astype(F32)
    perm = to == key_row
    local_row = (owner_row - group_row * group - group).astype(F32)
    local_col = jnp.sum(jnp.where(perm, local_row, 0.0), axis=1, keepdims=True) + group
    meta_out[...] = (
        jnp.broadcast_to(local_col, (sorted_slots, LANES))
        .astype(BF16)
        .reshape(nx, CAP, LANES)
    )
    elem_row = elem[...].astype(F32) + 1.0
    elem_col = jnp.sum(jnp.where(perm, elem_row, 0.0), axis=1, keepdims=True) - 1.0
    area_col = jnp.sum(jnp.where(perm, area[...], 0.0), axis=1, keepdims=True)
    for p in range(ex):
        at = lax.broadcasted_iota(jnp.int32, (sorted_slots, plane), 1) + p * plane
        pick[:, p * plane : (p + 1) * plane] = jnp.where(
            elem_col == at.astype(F32), 1.0, 0.0
        ).astype(BF16)

    def to_x(out, into, send_sem, recv_sem):
        return [
            pltpu.make_async_remote_copy(
                out.at[peer],
                into.at[gx],
                send_sem,
                recv_sem,
                device_id=(peer, gy),
                device_id_type=MESH,
            )
            for peer in x_peers
        ]

    def to_y():
        return [
            pltpu.make_async_remote_copy(
                sums_out.at[peer],
                sums_in.at[gy],
                sums_send,
                sums_recv,
                device_id=(gx, peer),
                device_id_type=MESH,
            )
            for peer in y_peers
        ]

    def wait_all(ref, n, sem):
        if n > 1:
            block = ref.at[pl.ds(0, n - 1)]
            pltpu.make_async_copy(block, block, sem).wait()

    for c in to_x(meta_out, meta_in, meta_send, meta_recv):
        c.start()
    meta_in[gx] = meta_out[gx]

    for c in block_copies:
        c.wait()
    last = [fb[f, :, body:width] for f in range(4)] + [
        sb[:, body:width],
        fb[4, :, body:width],
        fb[5, :, body:width],
        jnp.zeros((width, tail), BF16),
    ]
    for j in range(4):
        ends[:, j * LANES : (j + 1) * LANES] = jnp.concatenate(
            last[2 * j : 2 * j + 2], axis=1
        )

    iz = lax.rem(lax.broadcasted_iota(jnp.int32, (deep, 1), 0), ez)
    first_z, last_z = iz == 0, iz == ez - 1

    def dot(a, b):
        return jnp.dot(a, b, preferred_element_type=F32)

    def flat(x):
        return x.reshape(deep, x.shape[-1])

    def below(x):
        return jnp.where(first_z, 0.0, pltpu.roll(x, 1, 0))

    def above(x):
        return jnp.where(last_z, 0.0, pltpu.roll(x, deep - 1, 0))

    for it in range(ITERS):
        for k in range(CUTS):
            end_out[k * depth + 1 : k * depth + 1 + depth, mid] = dot(
                flat(near[k * depth + 1 : k * depth + 1 + depth, mid]), ends[...]
            ).reshape(depth, plane, 4 * LANES)

        if it == 0:
            ss_copy.wait()
            src_copy.wait()
        for k in range(CUTS):
            rows = pl.ds(k * depth, depth)
            here = (pl.ds(k * depth + 1, depth), mid)
            two = flat(end_out[(*here, slice(2 * LANES, 3 * LANES))])
            total[rows, :, 0:body] = src[rows, :, 0:body] - ss[rows, :, 0:body].astype(
                F32
            ) * dot(flat(near[here]), sb[:, 0:body]).reshape(depth, plane, body)
            total[rows, :, body:width] = src[rows, :, body:width] - ss[
                rows, :, body:width
            ].astype(F32) * two[:, 0:tail].reshape(depth, plane, tail)
        if it == 0:
            for c in [fs_copies[1], fs_copies[2], fs_copies[3], rx_copy]:
                c.start()
        for f in face_order:
            if it == 0:
                fs_copies[f].wait()
            for k in range(CUTS):
                p = k * depth
                rows = pl.ds(p, depth)
                if f < 4:
                    place = (
                        (pl.ds(p, depth), mid),
                        (pl.ds(p + 2, depth), mid),
                        (pl.ds(p + 1, depth), pl.ds(0, plane)),
                        (pl.ds(p + 1, depth), pl.ds(2 * ez, plane)),
                    )[f]
                    face = flat(near[place])
                    j = f // 2
                    end = flat(end_out[(*place, slice(j * LANES, (j + 1) * LANES))])
                    end = end[:, 0:tail] if f % 2 == 0 else end[:, tail : 2 * tail]
                else:
                    shift = below if f == 4 else above
                    face = shift(flat(adj[rows])).astype(BF16)
                    j = f - 2
                    end = shift(
                        flat(
                            end_out[
                                p + 1 : p + 1 + depth,
                                mid,
                                j * LANES : (j + 1) * LANES,
                            ]
                        )
                    )
                    end = end[:, tail : 2 * tail] if f == 4 else end[:, 0:tail]
                total[rows, :, 0:body] -= fs[f, rows, :, 0:body].astype(F32) * dot(
                    face, fb[f, :, 0:body]
                ).reshape(depth, plane, body)
                total[rows, :, body:width] -= fs[f, rows, :, body:width].astype(
                    F32
                ) * end.reshape(depth, plane, tail)

        if it == 0:
            rx_copy.wait()

        def renew(area):
            update = [
                (rx[a].astype(F32) * total[a]).astype(BF16).reshape(-1, width)
                for a in area
            ]
            step = dot(jnp.concatenate(update, axis=0), ib[...])
            start = 0
            for a, u in zip(area, update):
                new = adj[a] + step[start : start + u.shape[0]].reshape(adj[a].shape)
                start += u.shape[0]
                adj[a] = new
                rows, columns = a
                near[
                    pl.ds(rows.start + 1, rows.size),
                    pl.ds(columns.start + ez, columns.size),
                ] = new.astype(BF16)

        renew(areas[0])
        arrive(it, x_sides, gx, nx)
        for side, p in enumerate((0, ex - 1)):
            total[p] = total[p] - fs[side, p].astype(F32) * dot(
                unpack(x_halo.at[it, side], plane), fb[side]
            )
        renew(areas[1])
        arrive(it, y_sides, gy, ny)
        for side, a in enumerate((low, high)):
            total[:, a] = total[:, a] - fs[2 + side, :, a].astype(F32) * dot(
                unpack(y_halo.at[it, side], ex * ez), fb[2 + side]
            ).reshape(ex, ez, width)
        renew(areas[2])
        if it < ITERS - 1:
            send_y(
                it + 1,
                near[1 : ex + 1, pl.ds(ez, ez)].reshape(strip),
                near[1 : ex + 1, pl.ds(plane, ez)].reshape(strip),
            )
            send_x(it + 1, near[1, mid], near[ex, mid])

    out_copy = pltpu.make_async_copy(adj, out_hbm, out_sem.at[0])
    out_copy.start()

    picked = jnp.zeros((sorted_slots, width), F32)
    for k in range(CUTS):
        picked = picked + dot(
            pick[:, k * deep : (k + 1) * deep],
            flat(near[1 + depth * k : 1 + depth * (k + 1), mid]),
        )
    proj = dot(picked.astype(BF16), basis[...])
    rows_out[...] = (proj * area_col).astype(BF16).reshape(nx, CAP, -1)
    for c in to_x(rows_out, rows_in, rows_send, rows_recv):
        c.start()
    rows_in[gx] = rows_out[gx]

    wait_all(meta_in, nx, meta_recv)
    patch = lax.broadcasted_iota(jnp.int32, (sorted_slots, LANES), 1).astype(F32)
    mark = jnp.where(
        meta_in[...].reshape(sorted_slots, LANES).astype(F32) == patch, 1.0, 0.0
    ).astype(BF16)
    wait_all(rows_in, nx, rows_recv)
    sums = lax.dot_general(
        mark,
        rows_in[...].reshape(sorted_slots, -1),
        (((0,), (0,)), ((), ())),
        preferred_element_type=F32,
    )
    sums_out[...] = sums[:group].reshape(ny, P_DEV, -1)
    for c in to_y():
        c.start()
    sums_in[gy] = sums_out[gy]

    out_copy.wait()
    for it in range(ITERS):
        sent(it, x_sides, gx, nx)
        sent(it, y_sides, gy, ny)
    wait_all(meta_out, nx, meta_send)
    wait_all(rows_out, nx, rows_send)
    wait_all(sums_out, ny, sums_send)
    wait_all(sums_in, ny, sums_recv)
    grad_ref[...] = jnp.sum(sums_in[...], axis=0)


def store(out, grad, out_hbm, grad_hbm, held, held_grad, in_sem, out_sem):
    parts = in_sem.shape[0] - 1
    size = out.shape[0] // parts
    cuts = [pl.ds(k * size, size) for k in range(parts)]
    into = [
        pltpu.make_async_copy(out.at[r], held.at[r], in_sem.at[k])
        for k, r in enumerate(cuts)
    ] + [pltpu.make_async_copy(grad, held_grad, in_sem.at[parts])]
    away = [
        pltpu.make_async_copy(held.at[r], out_hbm.at[r], out_sem.at[k])
        for k, r in enumerate(cuts)
    ] + [pltpu.make_async_copy(held_grad, grad_hbm, out_sem.at[parts])]
    for c in into:
        c.start()
    for c, d in zip(into, away):
        c.wait()
        d.start()
    for d in away:
        d.wait()


def local(nx, ny, adjoint, source, ss, rx, fs, sb, fb, ib, basis, elem, owner, area):
    ex, ey, ez, width = adjoint.shape
    plane = ey * ez
    slots = elem.shape[2]
    params = basis.shape[1]
    planes = (ex, plane, width)
    vmem, dma = pltpu.VMEM, pltpu.SemaphoreType.DMA
    anywhere = pl.BlockSpec(memory_space=pl.ANY)
    out, grad = pl.pallas_call(
        functools.partial(kernel, nx, ny, ex, ey, ez),
        out_shape=(
            jax.ShapeDtypeStruct(planes, F32),
            jax.ShapeDtypeStruct((P_DEV, params), F32),
        ),
        in_specs=[anywhere] * 12,
        out_specs=(anywhere, pl.BlockSpec(memory_space=pltpu.VMEM)),
        scratch_shapes=[
            vmem(planes, F32),
            vmem(planes, F32),
            vmem(planes, BF16),
            vmem(planes, BF16),
            vmem((6, *planes), BF16),
            vmem(sb.shape, BF16),
            vmem(fb.shape, BF16),
            vmem(ib.shape, BF16),
            vmem(basis.shape, BF16),
            vmem((1, slots), jnp.int32),
            vmem((1, slots), jnp.int32),
            vmem((1, slots), F32),
            vmem((ex + 2, plane + 2 * ez, width), BF16),
            vmem(planes, F32),
            vmem((width, 4 * LANES), BF16),
            vmem((ex + 2, plane + 2 * ez, 4 * LANES), F32),
            vmem((ITERS, 2, plane * width // LANES, LANES), BF16),
            vmem((ITERS, 2, plane * width // LANES, LANES), BF16),
            vmem((ITERS, 2, ex * ez * width // LANES, LANES), BF16),
            vmem((ITERS, 2, ex * ez * width // LANES, LANES), BF16),
            vmem((nx * CAP, ex * plane), BF16),
            vmem((nx, CAP, LANES), BF16),
            vmem((nx, CAP, LANES), BF16),
            vmem((nx, CAP, params), BF16),
            vmem((nx, CAP, params), BF16),
            vmem((ny, P_DEV, params), F32),
            vmem((ny, P_DEV, params), F32),
            dma((3,)),
            dma((9,)),
            dma((4,)),
            dma((3,)),
            dma((3,)),
            dma((ITERS, 2)),
            dma((ITERS, 2)),
            dma((ITERS, 2)),
            dma((ITERS, 2)),
            dma,
            dma,
            dma,
            dma,
            dma,
            dma,
        ],
        compiler_params=pltpu.CompilerParams(
            collective_id=0 if nx * ny > 1 else None,
            has_side_effects=True,
            vmem_limit_bytes=62 * 1024 * 1024,
        ),
        name="sweeps",
    )(
        adjoint.reshape(planes),
        source.reshape(planes),
        ss.reshape(planes),
        rx.reshape(planes),
        fs.reshape(6, *planes),
        sb,
        fb,
        ib,
        basis,
        elem.reshape(1, slots),
        owner.reshape(1, slots),
        area.reshape(1, slots),
    )
    hbm = pl.BlockSpec(memory_space=pltpu.HBM)
    out, grad = pl.pallas_call(
        store,
        out_shape=(
            jax.ShapeDtypeStruct(planes, F32),
            jax.ShapeDtypeStruct((P_DEV, params), F32),
        ),
        in_specs=[anywhere] * 2,
        out_specs=(hbm, hbm),
        scratch_shapes=[
            vmem(planes, F32),
            vmem(grad.shape, F32),
            dma((5,)),
            dma((5,)),
        ],
        name="store",
    )(out, grad)
    return out.reshape(adjoint.shape), grad


def solution(mesh):
    return jax.shard_map(
        functools.partial(local, mesh.shape["gx"], mesh.shape["gy"]),
        mesh=mesh,
        in_specs=(
            P("gx", "gy", None, None),
            P("gx", "gy", None, None),
            P("gx", "gy", None, None),
            P("gx", "gy", None, None),
            P(None, "gx", "gy", None, None),
            P(),
            P(),
            P(),
            P(),
            P("gx", "gy", None),
            P("gx", "gy", None),
            P("gx", "gy", None),
        ),
        out_specs=(P("gx", "gy", None, None), P(("gx", "gy"), None)),
        check_vma=False,
    )
```

```python
import functools

import jax
import jax.numpy as jnp
from jax import lax
from jax.experimental import pallas as pl
from jax.experimental.pallas import tpu as pltpu
from jax.sharding import PartitionSpec as P

ITERS = 2
P_DEV = 8
CAP = 16
CUTS = 2
LANES = 128
MESH = pl.DeviceIdType.MESH
F32 = jnp.float32
BF16 = jnp.bfloat16


def offsets(n, parts):
    if n != functools.reduce(lambda a, b: a * b, (size for size, _ in parts), 1):
        parts = ((n, 1),)
    steps = [()]
    for size, _ in parts:
        steps = [(*o, d) for o in steps for d in range(size)]

    def far(o):
        return sum(min(d, m - d) * hops for d, (m, hops) in zip(o, parts))

    return parts, sorted([o for o in steps if any(o)], key=lambda o: -far(o))


def peers(me, n, parts):
    parts, steps = offsets(n, parts)
    coords, rest = [], me
    for size, _ in reversed(parts):
        coords.insert(0, lax.rem(rest, size))
        rest = rest // size
    out = []
    for o in steps:
        peer = 0
        for c, d, (size, _) in zip(coords, o, parts):
            peer = peer * size + (lax.rem(c + d, size) if d else c)
        out.append(peer)
    return out


def kernel(
    nx,
    ny,
    ex,
    ey,
    ez,
    adj_hbm,
    src_hbm,
    ss_hbm,
    rx_hbm,
    fs_hbm,
    sb_hbm,
    fb_hbm,
    ib_hbm,
    basis_hbm,
    elem_hbm,
    owner_hbm,
    area_hbm,
    adj,
    grad_ref,
    src,
    ss,
    rx,
    fs,
    sb,
    fb,
    ib,
    basis,
    elem,
    owner,
    area,
    near,
    total,
    ends,
    end_out,
    x_out,
    x_halo,
    y_out,
    y_halo,
    pick,
    meta_out,
    meta_in,
    rows_out,
    rows_in,
    sums_out,
    sums_in,
    adj_sem,
    plane_sem,
    block_sem,
    wall_sem,
    x_send,
    x_recv,
    y_send,
    y_recv,
    meta_send,
    meta_recv,
    rows_send,
    rows_recv,
    sums_send,
    sums_recv,
):
    gx, gy = lax.axis_index("gx"), lax.axis_index("gy")
    plane = ey * ez
    depth = ex // CUTS
    deep = depth * plane
    width = adj.shape[2]
    body = width // 256 * 256
    tail = width - body
    group = P_DEV * ny
    slots = elem.shape[1]
    sorted_slots = nx * CAP
    mid = pl.ds(ez, plane)
    x_peers = peers(gx, nx, ((2, 1), (4, 1), (2, 0.1)))
    y_peers = peers(gy, ny, ((4, 2), (4, 1)))

    low, high = pl.ds(0, ez), pl.ds(plane - ez, ez)
    inner = pl.ds(ez, plane - 2 * ez)
    adj_copies = [
        pltpu.make_async_copy(adj_hbm.at[:, a], adj.at[:, a], adj_sem.at[i])
        for i, a in enumerate((low, high, inner))
    ]
    wall_copies = [
        pltpu.make_async_copy(a, b, wall_sem.at[i])
        for i, (a, b) in enumerate(
            ((elem_hbm, elem), (owner_hbm, owner), (area_hbm, area))
        )
    ]
    block_copies = [
        pltpu.make_async_copy(a, b, block_sem.at[i])
        for i, (a, b) in enumerate(
            ((sb_hbm, sb), (fb_hbm, fb), (ib_hbm, ib), (basis_hbm, basis))
        )
    ]

    src_copy = pltpu.make_async_copy(src_hbm, src, plane_sem.at[0])
    ss_copy = pltpu.make_async_copy(ss_hbm, ss, plane_sem.at[1])
    rx_copy = pltpu.make_async_copy(rx_hbm, rx, plane_sem.at[2])
    fs_copies = [
        pltpu.make_async_copy(fs_hbm.at[f], fs.at[f], plane_sem.at[3 + f])
        for f in range(6)
    ]
    face_order = (4, 5, 0, 1, 2, 3)

    areas = (
        ((pl.ds(1, ex - 2), inner),),
        ((pl.ds(0, 1), inner), (pl.ds(ex - 1, 1), inner)),
        ((pl.ds(0, ex), low), (pl.ds(0, ex), high)),
    )

    for c in [*adj_copies, *block_copies, *wall_copies, ss_copy, src_copy]:
        c.start()

    if nx * ny > 1:
        barrier = pltpu.get_barrier_semaphore()
        for peer in x_peers:
            pl.semaphore_signal(
                barrier, inc=1, device_id=(peer, gy), device_id_type=MESH
            )
        for peer in y_peers:
            pl.semaphore_signal(
                barrier, inc=1, device_id=(gx, peer), device_id_type=MESH
            )

    zeros = jnp.zeros((ex, ez, width), BF16)
    near[0, mid] = jnp.zeros((plane, width), BF16)
    near[ex + 1, mid] = jnp.zeros((plane, width), BF16)
    near[1 : ex + 1, 0:ez] = zeros
    near[1 : ex + 1, ez + plane : 2 * ez + plane] = zeros
    end_zeros = jnp.zeros((ex, ez, 256), F32)
    end_out[0, mid, 0:256] = jnp.zeros((plane, 256), F32)
    end_out[ex + 1, mid, 0:256] = jnp.zeros((plane, 256), F32)
    end_out[1 : ex + 1, 0:ez, 0:256] = end_zeros
    end_out[1 : ex + 1, ez + plane : 2 * ez + plane, 0:256] = end_zeros
    rows_x = plane * width // LANES
    rows_y = ex * ez * width // LANES
    for it in range(ITERS):

        @pl.when(gx == 0)
        def _():
            x_halo[it, 0] = jnp.zeros((rows_x, LANES), BF16)

        @pl.when(gx == nx - 1)
        def _():
            x_halo[it, 1] = jnp.zeros((rows_x, LANES), BF16)

        @pl.when(gy == 0)
        def _():
            y_halo[it, 0] = jnp.zeros((rows_y, LANES), BF16)

        @pl.when(gy == ny - 1)
        def _():
            y_halo[it, 1] = jnp.zeros((rows_y, LANES), BF16)

    def pack(ref, x):
        n = x.shape[0]
        for j in range(body // LANES):
            ref[j * n : (j + 1) * n] = x[:, j * LANES : (j + 1) * LANES]
        end = x[:, body:width]
        ref[body // LANES * n : width * n // LANES] = jnp.concatenate(
            [end[: n // 2], end[n // 2 :]], axis=1
        )

    def unpack(ref, n):
        end = ref[body // LANES * n : width * n // LANES]
        return jnp.concatenate(
            [ref[j * n : (j + 1) * n] for j in range(body // LANES)]
            + [jnp.concatenate([end[:, 0:tail], end[:, tail : 2 * tail]], axis=0)],
            axis=1,
        )

    def sides(it, out, into, send_sem, recv_sem, ids):
        return [
            pltpu.make_async_remote_copy(
                out.at[it, i],
                into.at[it, i],
                send_sem.at[it, i],
                recv_sem.at[it, i],
                device_id=d,
                device_id_type=MESH,
            )
            for i, d in enumerate(ids)
        ]

    def x_sides(it):
        ids = ((jnp.minimum(gx + 1, nx - 1), gy), (jnp.maximum(gx - 1, 0), gy))
        return sides(it, x_out, x_halo, x_send, x_recv, ids)

    def y_sides(it):
        ids = ((gx, jnp.minimum(gy + 1, ny - 1)), (gx, jnp.maximum(gy - 1, 0)))
        return sides(it, y_out, y_halo, y_send, y_recv, ids)

    def send(it, make, me, n):
        up, down = make(it)
        pl.when(me < n - 1)(up.start)
        pl.when(me > 0)(down.start)

    def sent(it, make, me, n):
        up, down = make(it)
        pl.when(me < n - 1)(up.wait_send)
        pl.when(me > 0)(down.wait_send)

    def arrive(it, make, me, n):
        up, down = make(it)
        pl.when(me > 0)(up.wait_recv)
        pl.when(me < n - 1)(down.wait_recv)

    def send_x(it, first, final):
        pack(x_out.at[it, 0], final)
        pack(x_out.at[it, 1], first)
        send(it, x_sides, gx, nx)

    def send_y(it, first, final):
        pack(y_out.at[it, 0], final)
        pack(y_out.at[it, 1], first)
        send(it, y_sides, gy, ny)

    strip = (ex * ez, width)
    adj_copies[0].wait()
    adj_copies[1].wait()
    if nx * ny > 1:
        pl.semaphore_wait(barrier, nx + ny - 2)
    send_y(
        0,
        adj[:, low].astype(BF16).reshape(strip),
        adj[:, high].astype(BF16).reshape(strip),
    )
    adj_copies[2].wait()
    send_x(0, adj[0].astype(BF16), adj[ex - 1].astype(BF16))
    for c in [fs_copies[4], fs_copies[5], fs_copies[0]]:
        c.start()
    for k in range(CUTS):
        near[1 + depth * k : 1 + depth * (k + 1), mid] = adj[
            depth * k : depth * (k + 1)
        ].astype(BF16)

    for c in wall_copies:
        c.wait()
    owner_row = owner[...]
    group_row = owner_row // group
    g_row = group_row.astype(F32)
    sub = lax.broadcasted_iota(jnp.int32, (slots, slots), 0)
    lane = lax.broadcasted_iota(jnp.int32, (slots, slots), 1)
    g_col = jnp.sum(jnp.where(sub == lane, g_row, 0.0), axis=1, keepdims=True)
    before = jnp.where((g_col == g_row) & (sub < lane), 1.0, 0.0)
    rank_row = jnp.sum(before, axis=0, keepdims=True)
    key_row = g_row * CAP + rank_row
    to = lax.broadcasted_iota(jnp.int32, (sorted_slots, slots), 0).astype(F32)
    perm = to == key_row
    local_row = (owner_row - group_row * group - group).astype(F32)
    local_col = jnp.sum(jnp.where(perm, local_row, 0.0), axis=1, keepdims=True) + group
    meta_out[...] = (
        jnp.broadcast_to(local_col, (sorted_slots, LANES))
        .astype(BF16)
        .reshape(nx, CAP, LANES)
    )
    elem_row = elem[...].astype(F32) + 1.0
    elem_col = jnp.sum(jnp.where(perm, elem_row, 0.0), axis=1, keepdims=True) - 1.0
    area_col = jnp.sum(jnp.where(perm, area[...], 0.0), axis=1, keepdims=True)
    for p in range(ex):
        at = lax.broadcasted_iota(jnp.int32, (sorted_slots, plane), 1) + p * plane
        pick[:, p * plane : (p + 1) * plane] = jnp.where(
            elem_col == at.astype(F32), 1.0, 0.0
        ).astype(BF16)

    def to_x(out, into, send_sem, recv_sem):
        return [
            pltpu.make_async_remote_copy(
                out.at[peer],
                into.at[gx],
                send_sem,
                recv_sem,
                device_id=(peer, gy),
                device_id_type=MESH,
            )
            for peer in x_peers
        ]

    def to_y():
        return [
            pltpu.make_async_remote_copy(
                sums_out.at[peer],
                sums_in.at[gy],
                sums_send,
                sums_recv,
                device_id=(gx, peer),
                device_id_type=MESH,
            )
            for peer in y_peers
        ]

    def wait_all(ref, n, sem):
        if n > 1:
            block = ref.at[pl.ds(0, n - 1)]
            pltpu.make_async_copy(block, block, sem).wait()

    for c in to_x(meta_out, meta_in, meta_send, meta_recv):
        c.start()
    meta_in[gx] = meta_out[gx]

    for c in block_copies:
        c.wait()
    last = [fb[f, :, body:width] for f in range(4)] + [
        sb[:, body:width],
        fb[4, :, body:width],
        fb[5, :, body:width],
        jnp.zeros((width, tail), BF16),
    ]
    for j in range(4):
        ends[:, j * LANES : (j + 1) * LANES] = jnp.concatenate(
            last[2 * j : 2 * j + 2], axis=1
        )

    iz = lax.rem(lax.broadcasted_iota(jnp.int32, (deep, 1), 0), ez)
    first_z, last_z = iz == 0, iz == ez - 1

    def dot(a, b):
        return jnp.dot(a, b, preferred_element_type=F32)

    def flat(x):
        return x.reshape(deep, x.shape[-1])

    def below(x):
        return jnp.where(first_z, 0.0, pltpu.roll(x, 1, 0))

    def above(x):
        return jnp.where(last_z, 0.0, pltpu.roll(x, deep - 1, 0))

    for it in range(ITERS):
        for k in range(CUTS):
            end_out[k * depth + 1 : k * depth + 1 + depth, mid] = dot(
                flat(near[k * depth + 1 : k * depth + 1 + depth, mid]), ends[...]
            ).reshape(depth, plane, 4 * LANES)

        if it == 0:
            ss_copy.wait()
            src_copy.wait()
        for k in range(CUTS):
            rows = pl.ds(k * depth, depth)
            here = (pl.ds(k * depth + 1, depth), mid)
            two = flat(end_out[(*here, slice(2 * LANES, 3 * LANES))])
            total[rows, :, 0:body] = src[rows, :, 0:body] - ss[rows, :, 0:body].astype(
                F32
            ) * dot(flat(near[here]), sb[:, 0:body]).reshape(depth, plane, body)
            total[rows, :, body:width] = src[rows, :, body:width] - ss[
                rows, :, body:width
            ].astype(F32) * two[:, 0:tail].reshape(depth, plane, tail)
        if it == 0:
            for c in [fs_copies[1], fs_copies[2], fs_copies[3], rx_copy]:
                c.start()
        for f in face_order:
            if it == 0:
                fs_copies[f].wait()
            for k in range(CUTS):
                p = k * depth
                rows = pl.ds(p, depth)
                if f < 4:
                    place = (
                        (pl.ds(p, depth), mid),
                        (pl.ds(p + 2, depth), mid),
                        (pl.ds(p + 1, depth), pl.ds(0, plane)),
                        (pl.ds(p + 1, depth), pl.ds(2 * ez, plane)),
                    )[f]
                    face = flat(near[place])
                    j = f // 2
                    end = flat(end_out[(*place, slice(j * LANES, (j + 1) * LANES))])
                    end = end[:, 0:tail] if f % 2 == 0 else end[:, tail : 2 * tail]
                else:
                    shift = below if f == 4 else above
                    face = shift(flat(adj[rows])).astype(BF16)
                    j = f - 2
                    end = shift(
                        flat(
                            end_out[
                                p + 1 : p + 1 + depth,
                                mid,
                                j * LANES : (j + 1) * LANES,
                            ]
                        )
                    )
                    end = end[:, tail : 2 * tail] if f == 4 else end[:, 0:tail]
                total[rows, :, 0:body] -= fs[f, rows, :, 0:body].astype(F32) * dot(
                    face, fb[f, :, 0:body]
                ).reshape(depth, plane, body)
                total[rows, :, body:width] -= fs[f, rows, :, body:width].astype(
                    F32
                ) * end.reshape(depth, plane, tail)

        if it == 0:
            rx_copy.wait()

        def renew(area):
            update = [
                (rx[a].astype(F32) * total[a]).astype(BF16).reshape(-1, width)
                for a in area
            ]
            step = dot(jnp.concatenate(update, axis=0), ib[...])
            start = 0
            for a, u in zip(area, update):
                new = adj[a] + step[start : start + u.shape[0]].reshape(adj[a].shape)
                start += u.shape[0]
                adj[a] = new
                rows, columns = a
                near[
                    pl.ds(rows.start + 1, rows.size),
                    pl.ds(columns.start + ez, columns.size),
                ] = new.astype(BF16)

        renew(areas[0])
        arrive(it, x_sides, gx, nx)
        for side, p in enumerate((0, ex - 1)):
            total[p] = total[p] - fs[side, p].astype(F32) * dot(
                unpack(x_halo.at[it, side], plane), fb[side]
            )
        renew(areas[1])
        arrive(it, y_sides, gy, ny)
        for side, a in enumerate((low, high)):
            total[:, a] = total[:, a] - fs[2 + side, :, a].astype(F32) * dot(
                unpack(y_halo.at[it, side], ex * ez), fb[2 + side]
            ).reshape(ex, ez, width)
        renew(areas[2])
        if it < ITERS - 1:
            send_y(
                it + 1,
                near[1 : ex + 1, pl.ds(ez, ez)].reshape(strip),
                near[1 : ex + 1, pl.ds(plane, ez)].reshape(strip),
            )
            send_x(it + 1, near[1, mid], near[ex, mid])

    picked = jnp.zeros((sorted_slots, width), F32)
    for k in range(CUTS):
        picked = picked + dot(
            pick[:, k * deep : (k + 1) * deep],
            flat(near[1 + depth * k : 1 + depth * (k + 1), mid]),
        )
    proj = dot(picked.astype(BF16), basis[...])
    rows_out[...] = (proj * area_col).astype(BF16).reshape(nx, CAP, -1)
    for c in to_x(rows_out, rows_in, rows_send, rows_recv):
        c.start()
    rows_in[gx] = rows_out[gx]

    wait_all(meta_in, nx, meta_recv)
    patch = lax.broadcasted_iota(jnp.int32, (sorted_slots, LANES), 1).astype(F32)
    mark = jnp.where(
        meta_in[...].reshape(sorted_slots, LANES).astype(F32) == patch, 1.0, 0.0
    ).astype(BF16)
    wait_all(rows_in, nx, rows_recv)
    sums = lax.dot_general(
        mark,
        rows_in[...].reshape(sorted_slots, -1),
        (((0,), (0,)), ((), ())),
        preferred_element_type=F32,
    )
    sums_out[...] = sums[:group].reshape(ny, P_DEV, -1)
    for c in to_y():
        c.start()
    sums_in[gy] = sums_out[gy]

    for it in range(ITERS):
        sent(it, x_sides, gx, nx)
        sent(it, y_sides, gy, ny)
    wait_all(meta_out, nx, meta_send)
    wait_all(rows_out, nx, rows_send)
    wait_all(sums_out, ny, sums_send)
    wait_all(sums_in, ny, sums_recv)
    grad_ref[...] = jnp.sum(sums_in[...], axis=0)


def store(out, grad, out_hbm, grad_hbm, sem):
    copies = [
        pltpu.make_async_copy(a, b, sem.at[i])
        for i, (a, b) in enumerate(((out, out_hbm), (grad, grad_hbm)))
    ]
    for c in copies:
        c.start()
    for c in copies:
        c.wait()


def local(nx, ny, adjoint, source, ss, rx, fs, sb, fb, ib, basis, elem, owner, area):
    ex, ey, ez, width = adjoint.shape
    plane = ey * ez
    slots = elem.shape[2]
    params = basis.shape[1]
    planes = (ex, plane, width)
    vmem, dma = pltpu.VMEM, pltpu.SemaphoreType.DMA
    anywhere = pl.BlockSpec(memory_space=pl.ANY)
    out, grad = pl.pallas_call(
        functools.partial(kernel, nx, ny, ex, ey, ez),
        out_shape=(vmem(planes, F32), vmem((P_DEV, params), F32)),
        in_specs=[anywhere] * 12,
        out_specs=(pl.BlockSpec(memory_space=pltpu.VMEM),) * 2,
        scratch_shapes=[
            vmem(planes, F32),
            vmem(planes, BF16),
            vmem(planes, BF16),
            vmem((6, *planes), BF16),
            vmem(sb.shape, BF16),
            vmem(fb.shape, BF16),
            vmem(ib.shape, BF16),
            vmem(basis.shape, BF16),
            vmem((1, slots), jnp.int32),
            vmem((1, slots), jnp.int32),
            vmem((1, slots), F32),
            vmem((ex + 2, plane + 2 * ez, width), BF16),
            vmem(planes, F32),
            vmem((width, 4 * LANES), BF16),
            vmem((ex + 2, plane + 2 * ez, 4 * LANES), F32),
            vmem((ITERS, 2, plane * width // LANES, LANES), BF16),
            vmem((ITERS, 2, plane * width // LANES, LANES), BF16),
            vmem((ITERS, 2, ex * ez * width // LANES, LANES), BF16),
            vmem((ITERS, 2, ex * ez * width // LANES, LANES), BF16),
            vmem((nx * CAP, ex * plane), BF16),
            vmem((nx, CAP, LANES), BF16),
            vmem((nx, CAP, LANES), BF16),
            vmem((nx, CAP, params), BF16),
            vmem((nx, CAP, params), BF16),
            vmem((ny, P_DEV, params), F32),
            vmem((ny, P_DEV, params), F32),
            dma((3,)),
            dma((9,)),
            dma((4,)),
            dma((3,)),
            dma((ITERS, 2)),
            dma((ITERS, 2)),
            dma((ITERS, 2)),
            dma((ITERS, 2)),
            dma,
            dma,
            dma,
            dma,
            dma,
            dma,
        ],
        compiler_params=pltpu.CompilerParams(
            collective_id=0 if nx * ny > 1 else None,
            has_side_effects=True,
            vmem_limit_bytes=62_000_000,
        ),
        name="sweeps",
    )(
        adjoint.reshape(planes),
        source.reshape(planes),
        ss.reshape(planes),
        rx.reshape(planes),
        fs.reshape(6, *planes),
        sb,
        fb,
        ib,
        basis,
        elem.reshape(1, slots),
        owner.reshape(1, slots),
        area.reshape(1, slots),
    )
    hbm = pl.BlockSpec(memory_space=pltpu.HBM)
    out, grad = pl.pallas_call(
        store,
        out_shape=(
            jax.ShapeDtypeStruct(planes, F32),
            jax.ShapeDtypeStruct((P_DEV, params), F32),
        ),
        in_specs=[pl.BlockSpec(memory_space=pltpu.VMEM)] * 2,
        out_specs=(hbm, hbm),
        scratch_shapes=[dma((2,))],
        compiler_params=pltpu.CompilerParams(vmem_limit_bytes=8 * 1024 * 1024),
        name="store",
    )(out, grad)
    return out.reshape(adjoint.shape), grad


def solution(mesh):
    return jax.shard_map(
        functools.partial(local, mesh.shape["gx"], mesh.shape["gy"]),
        mesh=mesh,
        in_specs=(
            P("gx", "gy", None, None),
            P("gx", "gy", None, None),
            P("gx", "gy", None, None),
            P("gx", "gy", None, None),
            P(None, "gx", "gy", None, None),
            P(),
            P(),
            P(),
            P(),
            P("gx", "gy", None),
            P("gx", "gy", None),
            P("gx", "gy", None),
        ),
        out_specs=(P("gx", "gy", None, None), P(("gx", "gy"), None)),
        check_vma=False,
    )
```

```python
import functools

import jax
import jax.numpy as jnp
from jax import lax
from jax.experimental import pallas as pl
from jax.experimental.pallas import tpu as pltpu
from jax.sharding import PartitionSpec as P

ITERS = 2
P_DEV = 8
CAP = 16
CUTS = 2
LANES = 128
MESH = pl.DeviceIdType.MESH
F32 = jnp.float32
BF16 = jnp.bfloat16


def offsets(n, parts):
    if n != functools.reduce(lambda a, b: a * b, (size for size, _ in parts), 1):
        parts = ((n, 1),)
    steps = [()]
    for size, _ in parts:
        steps = [(*o, d) for o in steps for d in range(size)]

    def far(o):
        return sum(min(d, m - d) * hops for d, (m, hops) in zip(o, parts))

    return parts, sorted([o for o in steps if any(o)], key=lambda o: -far(o))


def peers(me, n, parts):
    parts, steps = offsets(n, parts)
    coords, rest = [], me
    for size, _ in reversed(parts):
        coords.insert(0, lax.rem(rest, size))
        rest = rest // size
    out = []
    for o in steps:
        peer = 0
        for c, d, (size, _) in zip(coords, o, parts):
            peer = peer * size + (lax.rem(c + d, size) if d else c)
        out.append(peer)
    return out


def kernel(
    nx,
    ny,
    ex,
    ey,
    ez,
    adj_hbm,
    src_hbm,
    ss_hbm,
    rx_hbm,
    fs_hbm,
    sb_hbm,
    fb_hbm,
    ib_hbm,
    basis_hbm,
    elem_hbm,
    owner_hbm,
    area_hbm,
    adj,
    grad_ref,
    src,
    ss,
    rx,
    fs,
    sb,
    fb,
    ib,
    basis,
    elem,
    owner,
    area,
    near,
    total,
    ends,
    end_out,
    x_out,
    x_halo,
    y_out,
    y_halo,
    pick,
    mark,
    meta_out,
    meta_in,
    rows_out,
    rows_in,
    sums_out,
    sums_in,
    adj_sem,
    plane_sem,
    block_sem,
    wall_sem,
    x_send,
    x_recv,
    y_send,
    y_recv,
    meta_send,
    meta_recv,
    rows_send,
    rows_recv,
    sums_send,
    sums_recv,
):
    gx, gy = lax.axis_index("gx"), lax.axis_index("gy")
    plane = ey * ez
    depth = ex // CUTS
    deep = depth * plane
    width = adj.shape[2]
    body = width // 256 * 256
    tail = width - body
    group = P_DEV * ny
    slots = elem.shape[1]
    sorted_slots = nx * CAP
    mid = pl.ds(ez, plane)
    x_peers = peers(gx, nx, ((2, 1), (4, 1), (2, 0.1)))
    y_peers = peers(gy, ny, ((4, 2), (4, 1)))

    low, high = pl.ds(0, ez), pl.ds(plane - ez, ez)
    inner = pl.ds(ez, plane - 2 * ez)
    adj_copies = [
        pltpu.make_async_copy(adj_hbm.at[:, a], adj.at[:, a], adj_sem.at[i])
        for i, a in enumerate((low, high, inner))
    ]
    wall_copies = [
        pltpu.make_async_copy(a, b, wall_sem.at[i])
        for i, (a, b) in enumerate(
            ((elem_hbm, elem), (owner_hbm, owner), (area_hbm, area))
        )
    ]
    block_copies = [
        pltpu.make_async_copy(a, b, block_sem.at[i])
        for i, (a, b) in enumerate(
            ((sb_hbm, sb), (fb_hbm, fb), (ib_hbm, ib), (basis_hbm, basis))
        )
    ]

    src_copy = pltpu.make_async_copy(src_hbm, src, plane_sem.at[0])
    ss_copy = pltpu.make_async_copy(ss_hbm, ss, plane_sem.at[1])
    rx_copy = pltpu.make_async_copy(rx_hbm, rx, plane_sem.at[2])
    fs_copies = [
        pltpu.make_async_copy(fs_hbm.at[f], fs.at[f], plane_sem.at[3 + f])
        for f in range(6)
    ]
    face_order = (4, 5, 0, 1, 2, 3)

    areas = (
        ((pl.ds(1, ex - 2), inner),),
        ((pl.ds(0, 1), inner), (pl.ds(ex - 1, 1), inner)),
        ((pl.ds(0, ex), low), (pl.ds(0, ex), high)),
    )

    for c in [*adj_copies, *block_copies, *wall_copies, ss_copy, src_copy]:
        c.start()

    if nx * ny > 1:
        barrier = pltpu.get_barrier_semaphore()
        for peer in x_peers:
            pl.semaphore_signal(
                barrier, inc=1, device_id=(peer, gy), device_id_type=MESH
            )
        for peer in y_peers:
            pl.semaphore_signal(
                barrier, inc=1, device_id=(gx, peer), device_id_type=MESH
            )

    zeros = jnp.zeros((ex, ez, width), BF16)
    near[0, mid] = jnp.zeros((plane, width), BF16)
    near[ex + 1, mid] = jnp.zeros((plane, width), BF16)
    near[1 : ex + 1, 0:ez] = zeros
    near[1 : ex + 1, ez + plane : 2 * ez + plane] = zeros
    end_zeros = jnp.zeros((ex, ez, 256), F32)
    end_out[0, mid, 0:256] = jnp.zeros((plane, 256), F32)
    end_out[ex + 1, mid, 0:256] = jnp.zeros((plane, 256), F32)
    end_out[1 : ex + 1, 0:ez, 0:256] = end_zeros
    end_out[1 : ex + 1, ez + plane : 2 * ez + plane, 0:256] = end_zeros
    rows_x = plane * width // LANES
    rows_y = ex * ez * width // LANES
    for it in range(ITERS):

        @pl.when(gx == 0)
        def _():
            x_halo[it, 0] = jnp.zeros((rows_x, LANES), BF16)

        @pl.when(gx == nx - 1)
        def _():
            x_halo[it, 1] = jnp.zeros((rows_x, LANES), BF16)

        @pl.when(gy == 0)
        def _():
            y_halo[it, 0] = jnp.zeros((rows_y, LANES), BF16)

        @pl.when(gy == ny - 1)
        def _():
            y_halo[it, 1] = jnp.zeros((rows_y, LANES), BF16)

    def pack(ref, x):
        n = x.shape[0]
        for j in range(body // LANES):
            ref[j * n : (j + 1) * n] = x[:, j * LANES : (j + 1) * LANES]
        end = x[:, body:width]
        ref[body // LANES * n : width * n // LANES] = jnp.concatenate(
            [end[: n // 2], end[n // 2 :]], axis=1
        )

    def unpack(ref, n):
        end = ref[body // LANES * n : width * n // LANES]
        return jnp.concatenate(
            [ref[j * n : (j + 1) * n] for j in range(body // LANES)]
            + [jnp.concatenate([end[:, 0:tail], end[:, tail : 2 * tail]], axis=0)],
            axis=1,
        )

    def sides(it, out, into, send_sem, recv_sem, ids):
        return [
            pltpu.make_async_remote_copy(
                out.at[it, i],
                into.at[it, i],
                send_sem.at[it, i],
                recv_sem.at[it, i],
                device_id=d,
                device_id_type=MESH,
            )
            for i, d in enumerate(ids)
        ]

    def x_sides(it):
        ids = ((jnp.minimum(gx + 1, nx - 1), gy), (jnp.maximum(gx - 1, 0), gy))
        return sides(it, x_out, x_halo, x_send, x_recv, ids)

    def y_sides(it):
        ids = ((gx, jnp.minimum(gy + 1, ny - 1)), (gx, jnp.maximum(gy - 1, 0)))
        return sides(it, y_out, y_halo, y_send, y_recv, ids)

    def send(it, make, me, n):
        up, down = make(it)
        pl.when(me < n - 1)(up.start)
        pl.when(me > 0)(down.start)

    def sent(it, make, me, n):
        up, down = make(it)
        pl.when(me < n - 1)(up.wait_send)
        pl.when(me > 0)(down.wait_send)

    def arrive(it, make, me, n):
        up, down = make(it)
        pl.when(me > 0)(up.wait_recv)
        pl.when(me < n - 1)(down.wait_recv)

    def send_x(it, first, final):
        pack(x_out.at[it, 0], final)
        pack(x_out.at[it, 1], first)
        send(it, x_sides, gx, nx)

    def send_y(it, first, final):
        up, down = y_sides(it)
        pack(y_out.at[it, 0], final)
        pl.when(gy < ny - 1)(up.start)
        pack(y_out.at[it, 1], first)
        pl.when(gy > 0)(down.start)

    strip = (ex * ez, width)
    adj_copies[0].wait()
    adj_copies[1].wait()
    if nx * ny > 1:
        pl.semaphore_wait(barrier, nx + ny - 2)
    send_y(
        0,
        adj[:, low].astype(BF16).reshape(strip),
        adj[:, high].astype(BF16).reshape(strip),
    )
    adj_copies[2].wait()
    send_x(0, adj[0].astype(BF16), adj[ex - 1].astype(BF16))
    for c in [fs_copies[4], fs_copies[5], fs_copies[0]]:
        c.start()

    for k in range(CUTS):
        near[1 + depth * k : 1 + depth * (k + 1), mid] = adj[
            depth * k : depth * (k + 1)
        ].astype(BF16)

    for c in wall_copies:
        c.wait()
    owner_row = owner[...]
    group_row = owner_row // group
    g_row = group_row.astype(F32)
    sub = lax.broadcasted_iota(jnp.int32, (slots, slots), 0)
    lane = lax.broadcasted_iota(jnp.int32, (slots, slots), 1)
    g_col = jnp.sum(jnp.where(sub == lane, g_row, 0.0), axis=1, keepdims=True)
    before = jnp.where((g_col == g_row) & (sub < lane), 1.0, 0.0)
    rank_row = jnp.sum(before, axis=0, keepdims=True)
    key_row = g_row * CAP + rank_row
    to = lax.broadcasted_iota(jnp.int32, (sorted_slots, slots), 0).astype(F32)
    perm = to == key_row
    local_row = (owner_row - group_row * group - group).astype(F32)
    local_col = jnp.sum(jnp.where(perm, local_row, 0.0), axis=1, keepdims=True) + group
    meta_out[...] = (
        jnp.broadcast_to(local_col, (sorted_slots, LANES))
        .astype(BF16)
        .reshape(nx, CAP, LANES)
    )
    elem_row = elem[...].astype(F32) + 1.0
    elem_col = jnp.sum(jnp.where(perm, elem_row, 0.0), axis=1, keepdims=True) - 1.0
    area_col = jnp.sum(jnp.where(perm, area[...], 0.0), axis=1, keepdims=True)
    most = plane - 2 * ez
    column = lax.broadcasted_iota(jnp.int32, (1, ex * plane), 1)
    on = column - ex * most
    off_at = column // most * plane + ez + lax.rem(column, most)
    on_low = on // ez * plane + lax.rem(on, ez)
    on_high = (on - ex * ez) // ez * plane + plane - ez + lax.rem(on, ez)
    at = jnp.where(on < 0, off_at, jnp.where(on < ex * ez, on_low, on_high))
    pick[...] = jnp.where(elem_col == at.astype(F32), 1.0, 0.0).astype(BF16)

    def to_x(out, into, send_sem, recv_sem):
        return [
            pltpu.make_async_remote_copy(
                out.at[peer],
                into.at[gx],
                send_sem,
                recv_sem,
                device_id=(peer, gy),
                device_id_type=MESH,
            )
            for peer in x_peers
        ]

    def to_y():
        return [
            pltpu.make_async_remote_copy(
                sums_out.at[peer],
                sums_in.at[gy],
                sums_send,
                sums_recv,
                device_id=(gx, peer),
                device_id_type=MESH,
            )
            for peer in y_peers
        ]

    def wait_all(ref, n, sem):
        if n > 1:
            block = ref.at[pl.ds(0, n - 1)]
            pltpu.make_async_copy(block, block, sem).wait()

    for c in to_x(meta_out, meta_in, meta_send, meta_recv):
        c.start()
    meta_in[gx] = meta_out[gx]

    for c in block_copies:
        c.wait()
    last = [fb[f, :, body:width] for f in range(4)] + [
        sb[:, body:width],
        fb[4, :, body:width],
        fb[5, :, body:width],
        jnp.zeros((width, tail), BF16),
    ]
    for j in range(4):
        ends[:, j * LANES : (j + 1) * LANES] = jnp.concatenate(
            last[2 * j : 2 * j + 2], axis=1
        )

    iz = lax.rem(lax.broadcasted_iota(jnp.int32, (deep, 1), 0), ez)
    first_z, last_z = iz == 0, iz == ez - 1

    def dot(a, b):
        return jnp.dot(a, b, preferred_element_type=F32)

    def flat(x):
        return x.reshape(deep, x.shape[-1])

    def below(x):
        return jnp.where(first_z, 0.0, pltpu.roll(x, 1, 0))

    def above(x):
        return jnp.where(last_z, 0.0, pltpu.roll(x, deep - 1, 0))

    for it in range(ITERS):
        for k in range(CUTS):
            end_out[k * depth + 1 : k * depth + 1 + depth, mid] = dot(
                flat(near[k * depth + 1 : k * depth + 1 + depth, mid]), ends[...]
            ).reshape(depth, plane, 4 * LANES)

        if it == 0:
            ss_copy.wait()
            src_copy.wait()
        for k in range(CUTS):
            rows = pl.ds(k * depth, depth)
            here = (pl.ds(k * depth + 1, depth), mid)
            two = flat(end_out[(*here, slice(2 * LANES, 3 * LANES))])
            total[rows, :, 0:body] = src[rows, :, 0:body] - ss[rows, :, 0:body].astype(
                F32
            ) * dot(flat(near[here]), sb[:, 0:body]).reshape(depth, plane, body)
            total[rows, :, body:width] = src[rows, :, body:width] - ss[
                rows, :, body:width
            ].astype(F32) * two[:, 0:tail].reshape(depth, plane, tail)
        if it == 0:
            for c in [fs_copies[1], fs_copies[2], fs_copies[3], rx_copy]:
                c.start()
        for f in face_order:
            if it == 0:
                fs_copies[f].wait()
            for k in range(CUTS):
                p = k * depth
                rows = pl.ds(p, depth)
                if f < 4:
                    place = (
                        (pl.ds(p, depth), mid),
                        (pl.ds(p + 2, depth), mid),
                        (pl.ds(p + 1, depth), pl.ds(0, plane)),
                        (pl.ds(p + 1, depth), pl.ds(2 * ez, plane)),
                    )[f]
                    face = flat(near[place])
                    j = f // 2
                    end = flat(end_out[(*place, slice(j * LANES, (j + 1) * LANES))])
                    end = end[:, 0:tail] if f % 2 == 0 else end[:, tail : 2 * tail]
                else:
                    shift = below if f == 4 else above
                    face = shift(flat(adj[rows])).astype(BF16)
                    j = f - 2
                    end = shift(
                        flat(
                            end_out[
                                p + 1 : p + 1 + depth,
                                mid,
                                j * LANES : (j + 1) * LANES,
                            ]
                        )
                    )
                    end = end[:, tail : 2 * tail] if f == 4 else end[:, 0:tail]
                total[rows, :, 0:body] -= fs[f, rows, :, 0:body].astype(F32) * dot(
                    face, fb[f, :, 0:body]
                ).reshape(depth, plane, body)
                total[rows, :, body:width] -= fs[f, rows, :, body:width].astype(
                    F32
                ) * end.reshape(depth, plane, tail)

        if it == 0:
            rx_copy.wait()

        def renew(area):
            update = [
                (rx[a].astype(F32) * total[a]).astype(BF16).reshape(-1, width)
                for a in area
            ]
            step = dot(jnp.concatenate(update, axis=0), ib[...])
            start = 0
            for a, u in zip(area, update):
                new = adj[a] + step[start : start + u.shape[0]].reshape(adj[a].shape)
                start += u.shape[0]
                adj[a] = new
                rows, columns = a
                near[
                    pl.ds(rows.start + 1, rows.size),
                    pl.ds(columns.start + ez, columns.size),
                ] = new.astype(BF16)

        renew(areas[0])
        arrive(it, x_sides, gx, nx)
        for side, p in enumerate((0, ex - 1)):
            total[p] = total[p] - fs[side, p].astype(F32) * dot(
                unpack(x_halo.at[it, side], plane), fb[side]
            )
        renew(areas[1])
        if it == ITERS - 1:
            picked = dot(
                pick[:, 0 : ex * most],
                near[1 : ex + 1, pl.ds(2 * ez, most)].reshape(-1, width),
            )
        arrive(it, y_sides, gy, ny)
        for side, a in enumerate((low, high)):
            total[:, a] = total[:, a] - fs[2 + side, :, a].astype(F32) * dot(
                unpack(y_halo.at[it, side], ex * ez), fb[2 + side]
            ).reshape(ex, ez, width)
        renew(areas[2])
        if it < ITERS - 1:
            send_y(
                it + 1,
                near[1 : ex + 1, pl.ds(ez, ez)].reshape(strip),
                near[1 : ex + 1, pl.ds(plane, ez)].reshape(strip),
            )
            send_x(it + 1, near[1, mid], near[ex, mid])

    for i, a in enumerate((pl.ds(ez, ez), pl.ds(plane, ez))):
        start = ex * (most + i * ez)
        picked = picked + dot(
            pick[:, start : start + ex * ez], near[1 : ex + 1, a].reshape(strip)
        )
    proj = dot(picked.astype(BF16), basis[...])
    rows_out[...] = (proj * area_col).astype(BF16).reshape(nx, CAP, -1)
    for c in to_x(rows_out, rows_in, rows_send, rows_recv):
        c.start()
    rows_in[gx] = rows_out[gx]

    wait_all(meta_in, nx, meta_recv)
    patch = lax.broadcasted_iota(jnp.int32, (sorted_slots, LANES), 1).astype(F32)
    mark[...] = jnp.where(
        meta_in[...].reshape(sorted_slots, LANES).astype(F32) == patch, 1.0, 0.0
    ).T.astype(BF16)
    wait_all(rows_in, nx, rows_recv)
    sums = dot(mark[...], rows_in[...].reshape(sorted_slots, -1))
    sums_out[...] = sums[:group].reshape(ny, P_DEV, -1)
    for c in to_y():
        c.start()
    sums_in[gy] = sums_out[gy]

    for it in range(ITERS):
        sent(it, x_sides, gx, nx)
        sent(it, y_sides, gy, ny)
    wait_all(meta_out, nx, meta_send)
    wait_all(rows_out, nx, rows_send)
    wait_all(sums_out, ny, sums_send)
    wait_all(sums_in, ny, sums_recv)
    grad_ref[...] = jnp.sum(sums_in[...], axis=0)


def store(out, grad, out_hbm, grad_hbm, sem):
    copies = [pltpu.make_async_copy(grad, grad_hbm, sem.at[out.shape[0]])] + [
        pltpu.make_async_copy(out.at[p], out_hbm.at[p], sem.at[p])
        for p in range(out.shape[0])
    ]
    for c in copies:
        c.start()
    for c in copies:
        c.wait()


def local(nx, ny, adjoint, source, ss, rx, fs, sb, fb, ib, basis, elem, owner, area):
    ex, ey, ez, width = adjoint.shape
    plane = ey * ez
    slots = elem.shape[2]
    params = basis.shape[1]
    planes = (ex, plane, width)
    vmem, dma = pltpu.VMEM, pltpu.SemaphoreType.DMA
    anywhere = pl.BlockSpec(memory_space=pl.ANY)
    out, grad = pl.pallas_call(
        functools.partial(kernel, nx, ny, ex, ey, ez),
        out_shape=(vmem(planes, F32), vmem((P_DEV, params), F32)),
        in_specs=[anywhere] * 12,
        out_specs=(pl.BlockSpec(memory_space=pltpu.VMEM),) * 2,
        scratch_shapes=[
            vmem(planes, F32),
            vmem(planes, BF16),
            vmem(planes, BF16),
            vmem((6, *planes), BF16),
            vmem(sb.shape, BF16),
            vmem(fb.shape, BF16),
            vmem(ib.shape, BF16),
            vmem(basis.shape, BF16),
            vmem((1, slots), jnp.int32),
            vmem((1, slots), jnp.int32),
            vmem((1, slots), F32),
            vmem((ex + 2, plane + 2 * ez, width), BF16),
            vmem(planes, F32),
            vmem((width, 4 * LANES), BF16),
            vmem((ex + 2, plane + 2 * ez, 4 * LANES), F32),
            vmem((ITERS, 2, plane * width // LANES, LANES), BF16),
            vmem((ITERS, 2, plane * width // LANES, LANES), BF16),
            vmem((ITERS, 2, ex * ez * width // LANES, LANES), BF16),
            vmem((ITERS, 2, ex * ez * width // LANES, LANES), BF16),
            vmem((nx * CAP, ex * plane), BF16),
            vmem((LANES, nx * CAP), BF16),
            vmem((nx, CAP, LANES), BF16),
            vmem((nx, CAP, LANES), BF16),
            vmem((nx, CAP, params), BF16),
            vmem((nx, CAP, params), BF16),
            vmem((ny, P_DEV, params), F32),
            vmem((ny, P_DEV, params), F32),
            dma((3,)),
            dma((9,)),
            dma((4,)),
            dma((3,)),
            dma((ITERS, 2)),
            dma((ITERS, 2)),
            dma((ITERS, 2)),
            dma((ITERS, 2)),
            dma,
            dma,
            dma,
            dma,
            dma,
            dma,
        ],
        compiler_params=pltpu.CompilerParams(
            collective_id=0 if nx * ny > 1 else None,
            has_side_effects=True,
            vmem_limit_bytes=62_000_000,
        ),
        name="sweeps",
    )(
        adjoint.reshape(planes),
        source.reshape(planes),
        ss.reshape(planes),
        rx.reshape(planes),
        fs.reshape(6, *planes),
        sb,
        fb,
        ib,
        basis,
        elem.reshape(1, slots),
        owner.reshape(1, slots),
        area.reshape(1, slots),
    )
    hbm = pl.BlockSpec(memory_space=pltpu.HBM)
    out, grad = pl.pallas_call(
        store,
        out_shape=(
            jax.ShapeDtypeStruct(planes, F32),
            jax.ShapeDtypeStruct((P_DEV, params), F32),
        ),
        in_specs=[pl.BlockSpec(memory_space=pltpu.VMEM)] * 2,
        out_specs=(hbm, hbm),
        scratch_shapes=[dma((ex + 1,))],
        compiler_params=pltpu.CompilerParams(vmem_limit_bytes=8 * 1024 * 1024),
        name="store",
    )(out, grad)
    return out.reshape(adjoint.shape), grad


def solution(mesh):
    return jax.shard_map(
        functools.partial(local, mesh.shape["gx"], mesh.shape["gy"]),
        mesh=mesh,
        in_specs=(
            P("gx", "gy", None, None),
            P("gx", "gy", None, None),
            P("gx", "gy", None, None),
            P("gx", "gy", None, None),
            P(None, "gx", "gy", None, None),
            P(),
            P(),
            P(),
            P(),
            P("gx", "gy", None),
            P("gx", "gy", None),
            P("gx", "gy", None),
        ),
        out_specs=(P("gx", "gy", None, None), P(("gx", "gy"), None)),
        check_vma=False,
    )
```
